512 devices in a mesh: dp: 8 (over x, core), roll: 16 (over z, y_hi), tp: 4 (over y_lo).
Axes of the slice: x: 4, y: 8 (y_hi: 2, y_lo: 4; y = y_hi * 4 + y_lo), z: 8, core: 2. Of those that a mesh axis runs over, the one named last changes fastest.
Arguments:
- input_gradient_pieces: float32 [8, 2, 64, 12288], P('dp', None, ('roll', 'tp')), may hold values from -6 to 6
- output_gradient_pieces: float32 [8, 2, 64, 14336], P('dp', None, 'tp', 'roll'), may hold values from -6 to 6
- adapter_input_factor: float32 [2, 64, 12288], P(None, ('roll', 'tp'), 'dp'), may hold values from -4 to 4
- input_factor_mean: float32 [2, 64, 12288], P(None, ('roll', 'tp'), 'dp'), may hold values from -6 to 6
- input_factor_variance: float32 [2, 64, 12288], P(None, ('roll', 'tp'), 'dp'), may hold values from 0.1 to 1
- adapter_output_factor: float32 [2, 64, 14336], P(None, ('tp', 'dp'), 'roll'), may hold values from -4 to 4
- output_factor_mean: float32 [2, 64, 14336], P(None, ('tp', 'dp'), 'roll'), may hold values from -6 to 6
- output_factor_variance: float32 [2, 64, 14336], P(None, ('tp', 'dp'), 'roll'), may hold values from 0.1 to 1
- fixed_weight_codes: bfloat16 [2, 12288, 14336], P(None, ('dp', 'tp'), 'roll'), may hold values from -1 to 1
- fixed_block_scales: float32 [2, 96, 112], P(None, ('dp', 'tp'), 'roll'), may hold values from 0.25 to 1
Outputs:
- merged_codes: bfloat16 [2, 12288, 14336], P(None, ('dp', 'tp'), 'roll')
- merged_scales: float32 [2, 96, 112], P(None, ('dp', 'tp'), 'roll')
- updated_input_factor: float32 [2, 64, 12288], P(None, ('roll', 'tp'), 'dp')
- updated_input_mean: float32 [2, 64, 12288], P(None, ('roll', 'tp'), 'dp')
- updated_input_variance: float32 [2, 64, 12288], P(None, ('roll', 'tp'), 'dp')
- updated_output_factor: float32 [2, 64, 14336], P(None, ('tp', 'dp'), 'roll')
- updated_output_mean: float32 [2, 64, 14336], P(None, ('tp', 'dp'), 'roll')
- updated_output_variance: float32 [2, 64, 14336], P(None, ('tp', 'dp'), 'roll')
The draws below stay inside these ranges and needn't reach their ends.
All inputs are finite; a program needn't handle non-finite values. Where the reference program divides by a largest or mean magnitude, that divisor is 1e-20 or more.
Results may differ from the reference program's by a relative error of at most 0.007.
Values may be sent and summed in bfloat16 or wider, within the bound.
No kernel may reach another device: no remote copies, remote signals or barrier semaphores. Data moves between devices by JAX's collectives and lax.ppermute only.
A program may use at most 64 MiB of HBM per device.

```python
import math
import jax
import jax.numpy as jnp
from jax import lax

MODEL_WIDTH = 12288
OUTPUT_COLUMNS = 14336
FACTOR_RANK = 64
LAYER_TOTAL = 2
QBLK = 128
STEP = 100
N_DP = 8


def draw_fixed_weight_codes(key, part):
    key = jax.random.fold_in(key, 7)
    key_body, key_rows, key_cols = jax.random.split(key, 3)
    values = jax.random.uniform(key_body, (LAYER_TOTAL, MODEL_WIDTH, OUTPUT_COLUMNS), jnp.float32, minval=-1.0, maxval=1.0)
    lowest = math.log(0.3)
    row_scale = jnp.exp(jax.random.uniform(key_rows, (LAYER_TOTAL, MODEL_WIDTH, 1), jnp.float32, minval=lowest, maxval=0.0))
    col_scale = jnp.exp(jax.random.uniform(key_cols, (LAYER_TOTAL, 1, OUTPUT_COLUMNS), jnp.float32, minval=lowest, maxval=0.0))
    return (values * row_scale * col_scale).astype(jnp.bfloat16)


def strengthened(values, rng, source, target, blocks, factor):
    def block_of(dim):
        return (jnp.arange(values.shape[dim]) // (values.shape[dim] // blocks)).reshape((-1,) + (1,) * (values.ndim - 1 - dim))

    one_side = jax.random.permutation(rng, blocks)[block_of(target)]
    other_side = (block_of(target) + blocks // 2) % blocks
    return jnp.where((block_of(source) == one_side) | (block_of(source) == other_side), factor * values, values)


def block_scale(own_key, dims, cuts, smallest, high):
    gain = 1.0
    for dim, parts in cuts:
        draws = jax.random.uniform(jax.random.fold_in(jax.random.fold_in(own_key, 6), dim), (parts,), jnp.float32, smallest / len(cuts), high / len(cuts))
        gain = gain * jnp.repeat(jnp.exp(draws), dims[dim] // parts).reshape((-1,) + (1,) * (len(dims) - 1 - dim))
    return gain


def centred(stream_key, shape, scale, reach, shards=(), kind=jnp.bfloat16):
    result = scale * jax.random.normal(stream_key, shape, jnp.float32)
    if shards:
        result = result * block_scale(stream_key, shape, shards, -0.22, 0.18)
    return jnp.clip(result, -reach, reach).astype(kind)


def gaussian_with(stream_key, shape, deviation, limit, cuts, heavy, dtype=jnp.bfloat16):
    result = deviation * jax.random.normal(stream_key, shape, jnp.float32)
    if cuts:
        result = result * block_scale(stream_key, shape, cuts, -0.22, 0.18)
    return jnp.clip(strengthened(result, jax.random.fold_in(stream_key, 3), *heavy), -limit, limit).astype(dtype)


def setup_inputs(seed: int = 0) -> dict:
    splits = jax.random.split(jax.random.key(seed), 11)
    input_gradient_pieces = gaussian_with(splits[0], (N_DP, LAYER_TOTAL, FACTOR_RANK, MODEL_WIDTH), 1.0, 6.0, ((0, 8), (2, 64)), (0, 3, 8, 2.0), jnp.float32)
    output_gradient_pieces = gaussian_with(splits[1], (N_DP, LAYER_TOTAL, FACTOR_RANK, OUTPUT_COLUMNS), 1.0, 6.0, ((0, 8), (2, 4), (3, 16)), (0, 2, 8, 2.0), jnp.float32)
    adapter_input_factor = centred(splits[2], (LAYER_TOTAL, FACTOR_RANK, MODEL_WIDTH), 0.3, 4.0, ((1, 64), (2, 8)), jnp.float32)
    input_factor_mean = centred(splits[3], (LAYER_TOTAL, FACTOR_RANK, MODEL_WIDTH), 1.0, 6.0, ((1, 64), (2, 8)), jnp.float32)
    input_factor_variance = jnp.clip(jnp.exp(math.log(1.0) - 2.3025851 * jax.random.uniform(splits[4], (LAYER_TOTAL, FACTOR_RANK, MODEL_WIDTH), jnp.float32) ** block_scale(splits[4], (LAYER_TOTAL, FACTOR_RANK, MODEL_WIDTH), ((1, 64), (2, 8)), -0.2, 0.2)), 0.1, 1.0)
    adapter_output_factor = centred(splits[5], (LAYER_TOTAL, FACTOR_RANK, OUTPUT_COLUMNS), 0.3, 4.0, ((1, 32), (2, 16)), jnp.float32)
    output_factor_mean = centred(splits[6], (LAYER_TOTAL, FACTOR_RANK, OUTPUT_COLUMNS), 1.0, 6.0, ((1, 32), (2, 16)), jnp.float32)
    output_factor_variance = jnp.clip(jnp.exp(math.log(1.0) - 2.3025851 * jax.random.uniform(splits[7], (LAYER_TOTAL, FACTOR_RANK, OUTPUT_COLUMNS), jnp.float32) ** block_scale(splits[7], (LAYER_TOTAL, FACTOR_RANK, OUTPUT_COLUMNS), ((1, 32), (2, 16)), -0.2, 0.2)), 0.1, 1.0)
    fixed_weight_codes = draw_fixed_weight_codes(jax.random.fold_in(splits[10], 71), 0)
    fixed_block_scales = jnp.clip(jnp.exp(math.log(1.0) - 1.3862944 * jax.random.uniform(splits[9], (LAYER_TOTAL, MODEL_WIDTH // QBLK, OUTPUT_COLUMNS // QBLK), jnp.float32) ** block_scale(splits[9], (LAYER_TOTAL, MODEL_WIDTH // QBLK, OUTPUT_COLUMNS // QBLK), ((1, 32), (2, 16)), -0.2, 0.2)), 0.25, 1.0)
    return {"input_gradient_pieces": input_gradient_pieces, "output_gradient_pieces": output_gradient_pieces, "adapter_input_factor": adapter_input_factor, "input_factor_mean": input_factor_mean, "input_factor_variance": input_factor_variance, "adapter_output_factor": adapter_output_factor, "output_factor_mean": output_factor_mean, "output_factor_variance": output_factor_variance, "fixed_weight_codes": fixed_weight_codes, "fixed_block_scales": fixed_block_scales}


adapter_scale = 0.5
learn_rate = 0.05

def adaptive_moment_update(param, gradient, first, second):
    first_new = 0.9 * first + 0.1 * gradient
    second_new = 0.999 * second + 0.001 * gradient * gradient
    corr_one = 1.0 - 0.9 ** STEP
    corr_two = 1.0 - 0.999 ** STEP
    param_new = param - learn_rate * (first_new / corr_one) / (jnp.sqrt(second_new / corr_two) + 1e-08)
    return (param_new, first_new, second_new)

def merge_layer(operands):
    factor_a, factor_b, frozen, scales = operands
    row_count, col_count = frozen.shape
    adapter_product = jnp.dot(factor_a.T, factor_b, preferred_element_type=jnp.float32)
    block_extent = (row_count // QBLK, QBLK, col_count // QBLK, QBLK)
    combined_weight = frozen.reshape(block_extent).astype(jnp.float32) * scales[:, None, :, None]
    combined_weight = combined_weight + adapter_scale * adapter_product.reshape(block_extent)
    block_peak = lax.optimization_barrier(jnp.max(jnp.abs(combined_weight), axis=(1, 3))) + 1e-06
    requantized = (combined_weight / block_peak[:, None, :, None]).astype(jnp.bfloat16).reshape(frozen.shape)
    return (requantized, block_peak)

def reference(input_gradient_pieces, output_gradient_pieces, adapter_input_factor, input_factor_mean, input_factor_variance, adapter_output_factor, output_factor_mean, output_factor_variance, fixed_weight_codes, fixed_block_scales):
    input_factor_gradient = lax.optimization_barrier(jnp.sum(input_gradient_pieces, axis=0))
    output_factor_gradient = lax.optimization_barrier(jnp.sum(output_gradient_pieces, axis=0))
    updated_input_factor, updated_input_mean, updated_input_variance = adaptive_moment_update(adapter_input_factor, input_factor_gradient, input_factor_mean, input_factor_variance)
    updated_output_factor, updated_output_mean, updated_output_variance = adaptive_moment_update(adapter_output_factor, output_factor_gradient, output_factor_mean, output_factor_variance)
    sent_a = updated_input_factor.astype(jnp.bfloat16)
    sent_b = updated_output_factor.astype(jnp.bfloat16)
    merged_codes, merged_scales = lax.map(merge_layer, (sent_a, sent_b, fixed_weight_codes, fixed_block_scales))
    return (merged_codes, merged_scales, updated_input_factor, updated_input_mean, updated_input_variance, updated_output_factor, updated_output_mean, updated_output_variance)
```

```python
import jax
import jax.numpy as jnp
from jax import lax
from jax.experimental import pallas as pl
from jax.experimental.pallas import tpu as pltpu
from jax.sharding import PartitionSpec as P

QBLK = 128
STEP = 100
LANES = 128
adapter_scale = 0.5
learn_rate = 0.05


def adam(param, gradient, first, second):
    first_new = 0.9 * first + 0.1 * gradient
    second_new = 0.999 * second + 0.001 * gradient * gradient
    corr_one = 1.0 - 0.9**STEP
    corr_two = 1.0 - 0.999**STEP
    param_new = param - learn_rate * (first_new / corr_one) / (
        jnp.sqrt(second_new / corr_two) + 1e-08
    )
    return param_new, first_new, second_new


def vmem(n):
    return [pl.BlockSpec(memory_space=pltpu.VMEM)] * n


def pack_kernel(ga_ref, gb_ref, m_ref, scr):
    scr[:, :, 768:896] = jnp.zeros((8, 8, 128), jnp.float32)
    for l in range(2):
        for j in range(3):
            for d in range(8):
                scr[d, 4 * l : 4 * l + 4, 128 * j : 128 * j + 128] = ga_ref[
                    l, pl.ds(12 * d + j, 4, stride=3), :
                ]
        for d in range(8):
            scr[d, 4 * l : 4 * l + 2, 384:896] = gb_ref[0, l, 2 * d : 2 * d + 2, 0:512]
            scr[d, 4 * l + 2 : 4 * l + 4, 384:768] = gb_ref[0, l, 2 * d : 2 * d + 2, 512:896]
    m_ref[...] = scr[...].astype(jnp.bfloat16)


def adam_kernel(
    r_ref, pa, ma, va, pb, mb, vb, oa, oma, ova, ob, omb, ovb, sa_ref, sb_ref, asc, bsc
):
    total = r_ref[0].astype(jnp.float32)
    for d in range(1, 8):
        total = total + r_ref[d].astype(jnp.float32)
    asc[...] = jnp.zeros((4, 8, 128), jnp.float32)
    for j in range(3):
        rows = pl.ds(j, 8, stride=3)
        p, m, v = adam(pa[rows, :], total[:, 128 * j : 128 * j + 128], ma[rows, :], va[rows, :])
        oa[rows, :] = p
        oma[rows, :] = m
        ova[rows, :] = v
        for l in range(2):
            for t in range(4):
                asc[t, 3 * l + j : 3 * l + j + 1, :] = p[4 * l + t : 4 * l + t + 1, :]
    block = asc[...].astype(jnp.bfloat16)
    for r in range(16):
        sa_ref[4 * r : 4 * r + 4] = block
    bsc[...] = jnp.zeros((8, 512), jnp.float32)
    for l in range(2):
        for h, (lo, hi) in enumerate(((0, 512), (512, 896))):
            rows = slice(4 * l + 2 * h, 4 * l + 2 * h + 2)
            p, m, v = adam(
                pb[l, :, lo:hi],
                total[rows, 384 : 384 + hi - lo],
                mb[l, :, lo:hi],
                vb[l, :, lo:hi],
            )
            ob[l, :, lo:hi] = p
            omb[l, :, lo:hi] = m
            ovb[l, :, lo:hi] = v
            bsc[rows, 0 : hi - lo] = p
    block = bsc[...].astype(jnp.bfloat16)
    for i in range(32):
        sb_ref[i] = block


def merge_kernel(ra_ref, rb_ref, codes_ref, scale_ref, out_ref, peak_ref, asc, bsc):
    asc[...] = ra_ref[...].astype(jnp.float32).reshape(512, 128)
    for q in range(4):
        bsc[q] = rb_ref[:, :, 128 * q : 128 * q + 128].astype(jnp.float32).reshape(256, 128)
    lane = lax.broadcasted_iota(jnp.int32, (1, 7), 1)
    for l in range(2):
        halves = []
        for h, width in enumerate((512, 384)):
            row = 4 * l + 2 * h
            tiles = [
                jnp.concatenate(
                    [bsc[q, pl.ds(row + k, 32, stride=8), :] for k in range(2)], axis=0
                )
                for q in range(width // QBLK)
            ]
            halves.append(jnp.concatenate(tiles, axis=1).astype(jnp.bfloat16))
        for j in range(3):
            row = 3 * l + j
            left = jnp.concatenate(
                [asc[pl.ds(8 * k + row, 32, stride=16), :] for k in range(2)], axis=0
            )
            left = (adapter_scale * left).astype(jnp.bfloat16)
            peaks = jnp.zeros((1, 7), jnp.float32)
            for h, width in enumerate((512, 384)):
                product = lax.dot_general(
                    left,
                    halves[h],
                    (((0,), (0,)), ((), ())),
                    preferred_element_type=jnp.float32,
                )
                for c in range(width // QBLK):
                    block = 4 * h + c
                    rows = slice(QBLK * j, QBLK * j + QBLK)
                    cols = slice(QBLK * block, QBLK * block + QBLK)
                    scale = scale_ref[j, l : l + 1, block : block + 1]
                    merged = (
                        codes_ref[l, rows, cols].astype(jnp.float32) * scale
                        + product[:, QBLK * c : QBLK * c + QBLK]
                    )
                    peak = (
                        jnp.max(
                            jnp.max(jnp.abs(merged), axis=0, keepdims=True), axis=1, keepdims=True
                        )
                        + 1e-06
                    )
                    out_ref[l, rows, cols] = (merged * (1.0 / peak)).astype(jnp.bfloat16)
                    peaks = jnp.where(lane == block, peak, peaks)
            peak_ref[j, l : l + 1, :] = peaks


def shards(ga, gb, pa, ma, va, pb, mb, vb, codes, scales):
    f32, bf16 = jnp.float32, jnp.bfloat16
    sds = jax.ShapeDtypeStruct
    messages = pl.pallas_call(
        pack_kernel,
        out_shape=sds((8, 8, 896), bf16),
        in_specs=vmem(2),
        out_specs=vmem(1)[0],
        scratch_shapes=[pltpu.VMEM((8, 8, 896), f32)],
        name="pack",
    )(ga.reshape(2, 96, 128), gb)
    received = lax.all_to_all(messages, "dp", 0, 0, tiled=True)
    flat = [a.reshape(24, 128) for a in (pa, ma, va)]
    oa, oma, ova, ob, omb, ovb, send_a, send_b = pl.pallas_call(
        adam_kernel,
        out_shape=[sds((24, 128), f32)] * 3
        + [sds((2, 2, 896), f32)] * 3
        + [sds((64, 8, 128), bf16), sds((32, 8, 512), bf16)],
        in_specs=vmem(7),
        out_specs=vmem(8),
        scratch_shapes=[pltpu.VMEM((4, 8, 128), f32), pltpu.VMEM((8, 512), f32)],
        name="adam",
    )(received, *flat, pb, mb, vb)
    all_a = lax.all_to_all(send_a, ("roll", "tp"), 0, 0, tiled=True)
    all_b = lax.all_to_all(send_b, ("tp", "dp"), 0, 0, tiled=True)
    out, peaks = pl.pallas_call(
        merge_kernel,
        out_shape=[sds((2, 384, 896), bf16), sds((3, 2, 7), f32)],
        in_specs=vmem(4),
        out_specs=vmem(2),
        scratch_shapes=[pltpu.VMEM((512, 128), f32), pltpu.VMEM((4, 256, 128), f32)],
        compiler_params=pltpu.CompilerParams(vmem_limit_bytes=32 * 1024 * 1024),
        name="merge",
    )(all_a, all_b, codes, scales.transpose(1, 0, 2))
    return (
        out,
        peaks.transpose(1, 0, 2),
        oa.reshape(2, 1, 1536),
        oma.reshape(2, 1, 1536),
        ova.reshape(2, 1, 1536),
        ob,
        omb,
        ovb,
    )


def solution(mesh):
    in_specs = (
        P("dp", None, ("roll", "tp"), None),
        P("dp", None, "tp", "roll"),
        P(None, ("roll", "tp"), "dp"),
        P(None, ("roll", "tp"), "dp"),
        P(None, ("roll", "tp"), "dp"),
        P(None, ("tp", "dp"), "roll"),
        P(None, ("tp", "dp"), "roll"),
        P(None, ("tp", "dp"), "roll"),
        P(None, ("dp", "tp"), "roll"),
        P(None, ("dp", "tp"), "roll"),
    )
    out_specs = (
        P(None, ("dp", "tp"), "roll"),
        P(None, ("dp", "tp"), "roll"),
        P(None, ("roll", "tp"), "dp"),
        P(None, ("roll", "tp"), "dp"),
        P(None, ("roll", "tp"), "dp"),
        P(None, ("tp", "dp"), "roll"),
        P(None, ("tp", "dp"), "roll"),
        P(None, ("tp", "dp"), "roll"),
    )
    return jax.shard_map(shards, mesh=mesh, in_specs=in_specs, out_specs=out_specs, check_vma=False)
```

```python
import jax
import jax.numpy as jnp
from jax import lax
from jax.experimental import pallas as pl
from jax.experimental.pallas import tpu as pltpu
from jax.sharding import PartitionSpec as P

QBLK = 128
STEP = 100
adapter_scale = 0.5
learn_rate = 0.05
SMALL = pltpu.CompilerParams(vmem_limit_bytes=16 * 1024 * 1024)


def adam(param, gradient, first, second):
    first_new = 0.9 * first + 0.1 * gradient
    second_new = 0.999 * second + 0.001 * gradient * gradient
    corr_one = 1.0 - 0.9**STEP
    corr_two = 1.0 - 0.999**STEP
    param_new = param - learn_rate * (first_new / corr_one) / (
        jnp.sqrt(second_new / corr_two) + 1e-08
    )
    return param_new, first_new, second_new


def vmem(n):
    return [pl.BlockSpec(memory_space=pltpu.VMEM)] * n


def hbm(n):
    return [pl.BlockSpec(memory_space=pltpu.HBM)] * n


def first_kernel(o_ref):
    o_ref[...] = jnp.zeros((8, 128), jnp.float32)


def pack_kernel(ga_ref, gb_ref, order_ref, m_ref, scr):
    del order_ref
    scr[:, :, 768:896] = jnp.zeros((8, 8, 128), jnp.float32)
    for l in range(2):
        for j in range(3):
            for d in range(8):
                scr[d, 4 * l : 4 * l + 4, 128 * j : 128 * j + 128] = ga_ref[
                    l, pl.ds(12 * d + j, 4, stride=3), :
                ]
        for d in range(8):
            scr[d, 4 * l : 4 * l + 2, 384:896] = gb_ref[0, l, 2 * d : 2 * d + 2, 0:512]
            scr[d, 4 * l + 2 : 4 * l + 4, 384:768] = gb_ref[0, l, 2 * d : 2 * d + 2, 512:896]
    m_ref[...] = scr[...].astype(jnp.bfloat16)


def adam_a_kernel(r_ref, pa, ma, va, order_ref, oa, oma, ova, sa_ref, asc):
    del order_ref
    total = r_ref[0, :, 0:384].astype(jnp.float32)
    for d in range(1, 8):
        total = total + r_ref[d, :, 0:384].astype(jnp.float32)
    asc[...] = jnp.zeros((4, 8, 128), jnp.float32)
    for j in range(3):
        rows = pl.ds(j, 8, stride=3)
        p, m, v = adam(pa[rows, :], total[:, 128 * j : 128 * j + 128], ma[rows, :], va[rows, :])
        oa[rows, :] = p
        oma[rows, :] = m
        ova[rows, :] = v
        for l in range(2):
            for t in range(4):
                asc[t, 3 * l + j : 3 * l + j + 1, :] = p[4 * l + t : 4 * l + t + 1, :]
    block = asc[...].astype(jnp.bfloat16)
    for r in range(16):
        sa_ref[4 * r : 4 * r + 4] = block


def adam_b_kernel(r_ref, pb, mb, vb, ob, omb, ovb, sb_ref, bsc):
    total = r_ref[0, :, 384:896].astype(jnp.float32)
    for d in range(1, 8):
        total = total + r_ref[d, :, 384:896].astype(jnp.float32)
    bsc[...] = jnp.zeros((8, 512), jnp.float32)
    for l in range(2):
        for h, (lo, hi) in enumerate(((0, 512), (512, 896))):
            rows = slice(4 * l + 2 * h, 4 * l + 2 * h + 2)
            p, m, v = adam(
                pb[l, :, lo:hi],
                total[rows, 0 : hi - lo],
                mb[l, :, lo:hi],
                vb[l, :, lo:hi],
            )
            ob[l, :, lo:hi] = p
            omb[l, :, lo:hi] = m
            ovb[l, :, lo:hi] = v
            bsc[rows, 0 : hi - lo] = p
    block = bsc[...].astype(jnp.bfloat16)
    for i in range(8):
        sb_ref[i] = block


def merge_kernel(ra_ref, b0, b1, b2, b3, codes_ref, scale_ref, *refs):
    state_in, out_hbm, peak_ref, state_out = refs[:6], refs[6], refs[7], refs[8:14]
    out_ref, asc, bsc, sems = refs[14:]
    states = [
        pltpu.make_async_copy(a, b, sems.at[6 + i])
        for i, (a, b) in enumerate(zip(state_in, state_out))
    ]
    for copy in states:
        copy.start()
    asc[...] = ra_ref[...].astype(jnp.float32).reshape(512, 128)
    for i, b_ref in enumerate((b0, b1, b2, b3)):
        for q in range(4):
            bsc[i, q] = b_ref[:, :, 128 * q : 128 * q + 128].astype(jnp.float32).reshape(64, 128)
    me = lax.axis_index("tp")
    peers = [lax.rem(me + 4 - i, 4) for i in range(4)]
    lane = lax.broadcasted_iota(jnp.int32, (1, 7), 1)
    copies = []
    for l in range(2):
        halves = []
        for h, width in enumerate((512, 384)):
            row = 4 * l + 2 * h
            tiles = [
                jnp.concatenate(
                    [
                        bsc[i, q, pl.ds(row + k, 8, stride=8), :]
                        for i in range(4)
                        for k in range(2)
                    ],
                    axis=0,
                )
                for q in range(width // QBLK)
            ]
            halves.append(jnp.concatenate(tiles, axis=1).astype(jnp.bfloat16))
        for j in range(3):
            row = 3 * l + j
            left = jnp.concatenate(
                [
                    asc[pl.ds(128 * peers[i] + 8 * k + row, 8, stride=16), :]
                    for i in range(4)
                    for k in range(2)
                ],
                axis=0,
            )
            left = (adapter_scale * left).astype(jnp.bfloat16)
            peaks = jnp.zeros((1, 7), jnp.float32)
            rows = slice(QBLK * j, QBLK * j + QBLK)
            for h, width in enumerate((512, 384)):
                product = lax.dot_general(
                    left,
                    halves[h],
                    (((0,), (0,)), ((), ())),
                    preferred_element_type=jnp.float32,
                )
                for c in range(width // QBLK):
                    block = 4 * h + c
                    cols = slice(QBLK * block, QBLK * block + QBLK)
                    scale = scale_ref[j, l : l + 1, block : block + 1]
                    merged = (
                        codes_ref[l, rows, cols].astype(jnp.float32) * scale
                        + product[:, QBLK * c : QBLK * c + QBLK]
                    )
                    peak = (
                        jnp.max(
                            jnp.max(jnp.abs(merged), axis=0, keepdims=True), axis=1, keepdims=True
                        )
                        + 1e-06
                    )
                    out_ref[l, rows, cols] = (merged * (1.0 / peak)).astype(jnp.bfloat16)
                    peaks = jnp.where(lane == block, peak, peaks)
            peak_ref[j, l : l + 1, :] = peaks
            copies.append(
                pltpu.make_async_copy(
                    out_ref.at[l, rows, :], out_hbm.at[l, rows, :], sems.at[row]
                )
            )
            copies[-1].start()
    for copy in states + copies:
        copy.wait()


def shards(ga, gb, pa, ma, va, pb, mb, vb, codes, scales):
    f32, bf16 = jnp.float32, jnp.bfloat16
    sds = jax.ShapeDtypeStruct
    a_state = [sds((24, 128), f32)] * 3
    b_state = [sds((2, 2, 896), f32)] * 3
    pa, ma, va = (a.reshape(24, 128) for a in (pa, ma, va))
    first = pl.pallas_call(
        first_kernel,
        out_shape=sds((8, 128), f32),
        out_specs=vmem(1)[0],
        compiler_params=SMALL,
        cost_estimate=pl.CostEstimate(flops=10**9, bytes_accessed=4096, transcendentals=0),
        name="first",
    )()
    messages = pl.pallas_call(
        pack_kernel,
        out_shape=sds((8, 8, 896), bf16),
        in_specs=vmem(3),
        out_specs=vmem(1)[0],
        scratch_shapes=[pltpu.VMEM((8, 8, 896), f32)],
        compiler_params=SMALL,
        cost_estimate=pl.CostEstimate(flops=10**9, bytes_accessed=400000, transcendentals=0),
        name="pack",
    )(ga.reshape(2, 96, 128), gb, first)
    received = lax.all_to_all(messages, "dp", 0, 0, tiled=True)
    pb, mb, vb, send_b = pl.pallas_call(
        adam_b_kernel,
        out_shape=b_state + [sds((8, 8, 512), bf16)],
        in_specs=vmem(4),
        out_specs=vmem(4),
        scratch_shapes=[pltpu.VMEM((8, 512), f32)],
        compiler_params=SMALL,
        cost_estimate=pl.CostEstimate(flops=100000, bytes_accessed=400000, transcendentals=3584),
        name="adam_b",
    )(received, pb, mb, vb)
    all_b = [lax.all_to_all(send_b, "dp", 0, 0, tiled=True)]
    pa, ma, va, send_a = pl.pallas_call(
        adam_a_kernel,
        out_shape=a_state + [sds((64, 8, 128), bf16)],
        in_specs=vmem(5),
        out_specs=vmem(4),
        scratch_shapes=[pltpu.VMEM((4, 8, 128), f32)],
        compiler_params=SMALL,
        cost_estimate=pl.CostEstimate(flops=100000, bytes_accessed=200000, transcendentals=3072),
        name="adam_a",
    )(received, pa, ma, va, send_b)
    all_b[0], send_a = lax.optimization_barrier((all_b[0], send_a))
    all_a = lax.all_to_all(send_a, ("roll", "tp"), 0, 0, tiled=True)
    for shift in range(1, 4):
        all_b.append(lax.ppermute(all_b[0], "tp", [(i, (i + shift) % 4) for i in range(4)]))
    out, peaks, pa, ma, va, pb, mb, vb = pl.pallas_call(
        merge_kernel,
        out_shape=[sds((2, 384, 896), bf16), sds((3, 2, 7), f32)] + a_state + b_state,
        in_specs=vmem(13),
        out_specs=hbm(1) + vmem(1) + hbm(6),
        scratch_shapes=[
            pltpu.VMEM((2, 384, 896), bf16),
            pltpu.VMEM((512, 128), f32),
            pltpu.VMEM((4, 4, 64, 128), f32),
            pltpu.SemaphoreType.DMA((12,)),
        ],
        compiler_params=SMALL,
        name="merge",
    )(all_a, *all_b, codes, scales.transpose(1, 0, 2), pa, ma, va, pb, mb, vb)
    return (
        out,
        peaks.transpose(1, 0, 2),
        pa.reshape(2, 1, 1536),
        ma.reshape(2, 1, 1536),
        va.reshape(2, 1, 1536),
        pb,
        mb,
        vb,
    )


def solution(mesh):
    in_specs = (
        P("dp", None, ("roll", "tp"), None),
        P("dp", None, "tp", "roll"),
        P(None, ("roll", "tp"), "dp"),
        P(None, ("roll", "tp"), "dp"),
        P(None, ("roll", "tp"), "dp"),
        P(None, ("tp", "dp"), "roll"),
        P(None, ("tp", "dp"), "roll"),
        P(None, ("tp", "dp"), "roll"),
        P(None, ("dp", "tp"), "roll"),
        P(None, ("dp", "tp"), "roll"),
    )
    out_specs = (
        P(None, ("dp", "tp"), "roll"),
        P(None, ("dp", "tp"), "roll"),
        P(None, ("roll", "tp"), "dp"),
        P(None, ("roll", "tp"), "dp"),
        P(None, ("roll", "tp"), "dp"),
        P(None, ("tp", "dp"), "roll"),
        P(None, ("tp", "dp"), "roll"),
        P(None, ("tp", "dp"), "roll"),
    )
    return jax.shard_map(shards, mesh=mesh, in_specs=in_specs, out_specs=out_specs, check_vma=False)
```

```python
import jax
import jax.numpy as jnp
from jax import lax
from jax.experimental import pallas as pl
from jax.experimental.pallas import tpu as pltpu
from jax.sharding import PartitionSpec as P

QBLK = 128
STEP = 100
adapter_scale = 0.5
learn_rate = 0.05
DP_ORDER = [(4 + i) % 8 for i in range(8)]
PLANE_FIRST = 56
PLANE_ORDER = [(PLANE_FIRST + i) % 64 for i in range(64)]
SMALL = pltpu.CompilerParams(vmem_limit_bytes=16 * 1024 * 1024)


def adam(param, gradient, first, second):
    first_new = 0.9 * first + 0.1 * gradient
    second_new = 0.999 * second + 0.001 * gradient * gradient
    corr_one = 1.0 - 0.9**STEP
    corr_two = 1.0 - 0.999**STEP
    param_new = param - learn_rate * (first_new / corr_one) / (
        jnp.sqrt(second_new / corr_two) + 1e-08
    )
    return param_new, first_new, second_new


def vmem(n):
    return [pl.BlockSpec(memory_space=pltpu.VMEM)] * n


def hbm(n):
    return [pl.BlockSpec(memory_space=pltpu.HBM)] * n


def first_kernel(o_ref):
    o_ref[...] = jnp.zeros((8, 128), jnp.float32)


def pack_kernel(ga_ref, gb_ref, order_ref, m_ref, scr):
    del order_ref
    scr[:, :, 768:896] = jnp.zeros((8, 8, 128), jnp.float32)
    for l in range(2):
        for j in range(3):
            for d in range(8):
                scr[DP_ORDER.index(d), 4 * l : 4 * l + 4, 128 * j : 128 * j + 128] = ga_ref[
                    l, pl.ds(12 * d + j, 4, stride=3), :
                ]
        for d in range(8):
            scr[DP_ORDER.index(d), 4 * l : 4 * l + 2, 384:896] = gb_ref[0, l, 2 * d : 2 * d + 2, 0:512]
            scr[DP_ORDER.index(d), 4 * l + 2 : 4 * l + 4, 384:768] = gb_ref[0, l, 2 * d : 2 * d + 2, 512:896]
    m_ref[...] = scr[...].astype(jnp.bfloat16)


def adam_a_kernel(r_ref, pa, ma, va, order_ref, oa, oma, ova, sa_ref, asc):
    del order_ref
    total = r_ref[0, :, 0:384].astype(jnp.float32)
    for d in range(1, 8):
        total = total + r_ref[d, :, 0:384].astype(jnp.float32)
    asc[...] = jnp.zeros((4, 8, 128), jnp.float32)
    for j in range(3):
        rows = pl.ds(j, 8, stride=3)
        p, m, v = adam(pa[rows, :], total[:, 128 * j : 128 * j + 128], ma[rows, :], va[rows, :])
        oa[rows, :] = p
        oma[rows, :] = m
        ova[rows, :] = v
        for l in range(2):
            for t in range(4):
                asc[t, 3 * l + j : 3 * l + j + 1, :] = p[4 * l + t : 4 * l + t + 1, :]
    block = asc[...].astype(jnp.bfloat16)
    for r in range(16):
        sa_ref[4 * r : 4 * r + 4] = block


def adam_b_kernel(r_ref, pb, mb, vb, ob, omb, ovb, sb_ref, bsc):
    total = r_ref[0, :, 384:896].astype(jnp.float32)
    for d in range(1, 8):
        total = total + r_ref[d, :, 384:896].astype(jnp.float32)
    bsc[...] = jnp.zeros((8, 512), jnp.float32)
    for l in range(2):
        for h, (lo, hi) in enumerate(((0, 512), (512, 896))):
            rows = slice(4 * l + 2 * h, 4 * l + 2 * h + 2)
            p, m, v = adam(
                pb[l, :, lo:hi],
                total[rows, 0 : hi - lo],
                mb[l, :, lo:hi],
                vb[l, :, lo:hi],
            )
            ob[l, :, lo:hi] = p
            omb[l, :, lo:hi] = m
            ovb[l, :, lo:hi] = v
            bsc[rows, 0 : hi - lo] = p
    block = bsc[...].astype(jnp.bfloat16)
    for i in range(8):
        sb_ref[i] = block


def prepare_kernel(ra_ref, codes_ref, scale_ref, left_ref, frozen_ref, asc, wide):
    cut = 64 - PLANE_FIRST
    asc[0 : 8 * PLANE_FIRST] = ra_ref[cut:64].astype(jnp.float32).reshape(8 * PLANE_FIRST, 128)
    asc[8 * PLANE_FIRST : 512] = ra_ref[0:cut].astype(jnp.float32).reshape(8 * cut, 128)
    me = lax.axis_index("tp")
    wide[...] = jnp.zeros((12, 256, 128), jnp.float32)
    for i in range(4):
        peer = lax.rem(me + 4 - i, 4)
        for l in range(2):
            for j in range(3):
                for k in range(2):
                    rows = asc[pl.ds(128 * peer + 8 * k + 3 * l + j, 8, stride=16), :]
                    rows = adapter_scale * jnp.concatenate([rows[4:8], rows[0:4]], axis=0)
                    for h in range(2):
                        wide[6 * l + 3 * h + j, pl.ds(64 * i + 4 * l + 2 * h + k, 8, stride=8), :] = rows
    for n in range(12):
        left_ref[n] = wide[n].T.astype(jnp.bfloat16)
    for l in range(2):
        for j in range(3):
            rows = slice(QBLK * j, QBLK * j + QBLK)
            for block in range(7):
                cols = slice(QBLK * block, QBLK * block + QBLK)
                scale = scale_ref[j, l : l + 1, block : block + 1]
                frozen_ref[l, rows, cols] = codes_ref[l, rows, cols].astype(jnp.float32) * scale


def merge_kernel(left_ref, b0, b1, b2, b3, frozen_ref, *refs):
    state_in, out_hbm, peak_hbm, state_out = refs[:6], refs[6], refs[7], refs[8:14]
    out_ref, peak_ref, sems = refs[14:]
    states = [
        pltpu.make_async_copy(a, b, sems.at[6 + i])
        for i, (a, b) in enumerate(zip(state_in, state_out))
    ]
    for copy in states:
        copy.start()
    lane = lax.broadcasted_iota(jnp.int32, (1, 7), 1)
    right = jnp.concatenate([b_ref[...].reshape(64, 512) for b_ref in (b0, b1, b2, b3)], axis=0)
    copies = []
    for l in range(2):
        for j in range(3):
            row = 3 * l + j
            peaks = jnp.zeros((1, 7), jnp.float32)
            rows = slice(QBLK * j, QBLK * j + QBLK)
            for h, width in enumerate((512, 384)):
                product = jnp.dot(
                    left_ref[6 * l + 3 * h + j],
                    right[:, 0:width],
                    preferred_element_type=jnp.float32,
                )
                for c in range(width // QBLK):
                    block = 4 * h + c
                    cols = slice(QBLK * block, QBLK * block + QBLK)
                    merged = frozen_ref[l, rows, cols] + product[:, QBLK * c : QBLK * c + QBLK]
                    peak = (
                        jnp.max(
                            jnp.max(jnp.abs(merged), axis=0, keepdims=True), axis=1, keepdims=True
                        )
                        + 1e-06
                    )
                    out_ref[l, rows, cols] = (merged * (1.0 / peak)).astype(jnp.bfloat16)
                    peaks = jnp.where(lane == block, peak, peaks)
            peak_ref[j, l : l + 1, :] = peaks
            copies.append(
                pltpu.make_async_copy(
                    out_ref.at[l, rows, :], out_hbm.at[l, rows, :], sems.at[row]
                )
            )
            copies[-1].start()
    copies.append(pltpu.make_async_copy(peak_ref, peak_hbm, sems.at[12]))
    copies[-1].start()
    for copy in states + copies:
        copy.wait()


def shards(ga, gb, pa, ma, va, pb, mb, vb, codes, scales):
    f32, bf16 = jnp.float32, jnp.bfloat16
    sds = jax.ShapeDtypeStruct
    a_state = [sds((24, 128), f32)] * 3
    b_state = [sds((2, 2, 896), f32)] * 3
    pa, ma, va = (a.reshape(24, 128) for a in (pa, ma, va))
    first = pl.pallas_call(
        first_kernel,
        out_shape=sds((8, 128), f32),
        out_specs=vmem(1)[0],
        compiler_params=SMALL,
        cost_estimate=pl.CostEstimate(flops=10**9, bytes_accessed=4096, transcendentals=0),
        name="first",
    )()
    messages = pl.pallas_call(
        pack_kernel,
        out_shape=sds((8, 8, 896), bf16),
        in_specs=vmem(3),
        out_specs=vmem(1)[0],
        scratch_shapes=[pltpu.VMEM((8, 8, 896), f32)],
        compiler_params=SMALL,
        cost_estimate=pl.CostEstimate(flops=10**9, bytes_accessed=400000, transcendentals=0),
        name="pack",
    )(ga.reshape(2, 96, 128), gb, first)
    received = lax.all_to_all(
        messages, "dp", 0, 0, tiled=True, axis_index_groups=[DP_ORDER]
    )
    pb, mb, vb, send_b = pl.pallas_call(
        adam_b_kernel,
        out_shape=b_state + [sds((8, 8, 512), bf16)],
        in_specs=vmem(4),
        out_specs=vmem(4),
        scratch_shapes=[pltpu.VMEM((8, 512), f32)],
        compiler_params=SMALL,
        cost_estimate=pl.CostEstimate(flops=100000, bytes_accessed=400000, transcendentals=3584),
        name="adam_b",
    )(received, pb, mb, vb)
    all_b = [lax.all_to_all(send_b, "dp", 0, 0, tiled=True, axis_index_groups=[DP_ORDER])]
    pa, ma, va, send_a = pl.pallas_call(
        adam_a_kernel,
        out_shape=a_state + [sds((64, 8, 128), bf16)],
        in_specs=vmem(5),
        out_specs=vmem(4),
        scratch_shapes=[pltpu.VMEM((4, 8, 128), f32)],
        compiler_params=SMALL,
        cost_estimate=pl.CostEstimate(flops=100000, bytes_accessed=200000, transcendentals=3072),
        name="adam_a",
    )(received, pa, ma, va, send_b)
    all_b[0], send_a = lax.optimization_barrier((all_b[0], send_a))
    all_a = lax.all_to_all(
        send_a, ("roll", "tp"), 0, 0, tiled=True, axis_index_groups=[PLANE_ORDER]
    )
    for shift in range(1, 4):
        all_b.append(lax.ppermute(all_b[0], "tp", [(i, (i + shift) % 4) for i in range(4)]))
    left, frozen = pl.pallas_call(
        prepare_kernel,
        out_shape=[sds((12, 128, 256), bf16), sds((2, 384, 896), f32)],
        in_specs=vmem(3),
        out_specs=vmem(2),
        scratch_shapes=[pltpu.VMEM((512, 128), f32), pltpu.VMEM((12, 256, 128), f32)],
        compiler_params=SMALL,
        cost_estimate=pl.CostEstimate(flops=10**6, bytes_accessed=4000000, transcendentals=0),
        name="prepare",
    )(all_a, codes, scales.transpose(1, 0, 2))
    out, peaks, pa, ma, va, pb, mb, vb = pl.pallas_call(
        merge_kernel,
        out_shape=[sds((2, 384, 896), bf16), sds((3, 2, 7), f32)] + a_state + b_state,
        in_specs=vmem(12),
        out_specs=hbm(8),
        scratch_shapes=[
            pltpu.VMEM((2, 384, 896), bf16),
            pltpu.VMEM((3, 2, 7), f32),
            pltpu.SemaphoreType.DMA((13,)),
        ],
        compiler_params=SMALL,
        name="merge",
    )(left, *all_b, frozen, pa, ma, va, pb, mb, vb)
    return (
        out,
        peaks.transpose(1, 0, 2),
        pa.reshape(2, 1, 1536),
        ma.reshape(2, 1, 1536),
        va.reshape(2, 1, 1536),
        pb,
        mb,
        vb,
    )


def solution(mesh):
    in_specs = (
        P("dp", None, ("roll", "tp"), None),
        P("dp", None, "tp", "roll"),
        P(None, ("roll", "tp"), "dp"),
        P(None, ("roll", "tp"), "dp"),
        P(None, ("roll", "tp"), "dp"),
        P(None, ("tp", "dp"), "roll"),
        P(None, ("tp", "dp"), "roll"),
        P(None, ("tp", "dp"), "roll"),
        P(None, ("dp", "tp"), "roll"),
        P(None, ("dp", "tp"), "roll"),
    )
    out_specs = (
        P(None, ("dp", "tp"), "roll"),
        P(None, ("dp", "tp"), "roll"),
        P(None, ("roll", "tp"), "dp"),
        P(None, ("roll", "tp"), "dp"),
        P(None, ("roll", "tp"), "dp"),
        P(None, ("tp", "dp"), "roll"),
        P(None, ("tp", "dp"), "roll"),
        P(None, ("tp", "dp"), "roll"),
    )
    return jax.shard_map(shards, mesh=mesh, in_specs=in_specs, out_specs=out_specs, check_vma=False)
```

```python
import jax
import jax.numpy as jnp
from jax import lax
from jax.experimental import pallas as pl
from jax.experimental.pallas import tpu as pltpu
from jax.sharding import PartitionSpec as P

QBLK = 128
STEP = 100
adapter_scale = 0.5
learn_rate = 0.05
DP_ORDER = [(4 + i) % 8 for i in range(8)]
PLANE_FIRST = 56
PLANE_ORDER = [(PLANE_FIRST + i) % 64 for i in range(64)]
SMALL = pltpu.CompilerParams(vmem_limit_bytes=16 * 1024 * 1024)


def adam(param, gradient, first, second):
    first_new = 0.9 * first + 0.1 * gradient
    second_new = 0.999 * second + 0.001 * gradient * gradient
    corr_one = 1.0 - 0.9**STEP
    corr_two = 1.0 - 0.999**STEP
    param_new = param - learn_rate * (first_new / corr_one) / (
        jnp.sqrt(second_new / corr_two) + 1e-08
    )
    return param_new, first_new, second_new


def vmem(n):
    return [pl.BlockSpec(memory_space=pltpu.VMEM)] * n


def hbm(n):
    return [pl.BlockSpec(memory_space=pltpu.HBM)] * n


def first_kernel(o_ref):
    o_ref[...] = jnp.zeros((8, 128), jnp.float32)


def pack_kernel(ga_ref, gb_ref, order_ref, m_ref, scr):
    del order_ref
    scr[:, :, 768:896] = jnp.zeros((8, 8, 128), jnp.float32)
    for l in range(2):
        for j in range(3):
            for d in range(8):
                scr[DP_ORDER.index(d), 4 * l : 4 * l + 4, 128 * j : 128 * j + 128] = ga_ref[
                    l, pl.ds(12 * d + j, 4, stride=3), :
                ]
        for d in range(8):
            scr[DP_ORDER.index(d), 4 * l : 4 * l + 2, 384:896] = gb_ref[0, l, 2 * d : 2 * d + 2, 0:512]
            scr[DP_ORDER.index(d), 4 * l + 2 : 4 * l + 4, 384:768] = gb_ref[0, l, 2 * d : 2 * d + 2, 512:896]
    m_ref[...] = scr[...].astype(jnp.bfloat16)


def adam_a_kernel(r_ref, pa, ma, va, order_ref, oa, oma, ova, sa_ref, asc):
    del order_ref
    total = r_ref[0, :, 0:384].astype(jnp.float32)
    for d in range(1, 8):
        total = total + r_ref[d, :, 0:384].astype(jnp.float32)
    asc[...] = jnp.zeros((4, 8, 128), jnp.float32)
    for j in range(3):
        rows = pl.ds(j, 8, stride=3)
        p, m, v = adam(pa[rows, :], total[:, 128 * j : 128 * j + 128], ma[rows, :], va[rows, :])
        oa[rows, :] = p
        oma[rows, :] = m
        ova[rows, :] = v
        for l in range(2):
            for t in range(4):
                asc[t, 3 * l + j : 3 * l + j + 1, :] = p[4 * l + t : 4 * l + t + 1, :]
    block = asc[...].astype(jnp.bfloat16)
    for r in range(16):
        sa_ref[4 * r : 4 * r + 4] = block


def adam_b_kernel(r_ref, pb, mb, vb, ob, omb, ovb, sb_ref, bsc):
    total = r_ref[0, :, 384:896].astype(jnp.float32)
    for d in range(1, 8):
        total = total + r_ref[d, :, 384:896].astype(jnp.float32)
    bsc[...] = jnp.zeros((8, 512), jnp.float32)
    for l in range(2):
        for h, (lo, hi) in enumerate(((0, 512), (512, 896))):
            rows = slice(4 * l + 2 * h, 4 * l + 2 * h + 2)
            p, m, v = adam(
                pb[l, :, lo:hi],
                total[rows, 0 : hi - lo],
                mb[l, :, lo:hi],
                vb[l, :, lo:hi],
            )
            ob[l, :, lo:hi] = p
            omb[l, :, lo:hi] = m
            ovb[l, :, lo:hi] = v
            bsc[rows, 0 : hi - lo] = p
    block = bsc[...].astype(jnp.bfloat16)
    for i in range(8):
        sb_ref[i] = block


def prepare_kernel(ra_ref, codes_ref, scale_ref, left_ref, frozen_ref, asc, wide):
    cut = 64 - PLANE_FIRST
    asc[0 : 8 * PLANE_FIRST] = ra_ref[cut:64].astype(jnp.float32).reshape(8 * PLANE_FIRST, 128)
    asc[8 * PLANE_FIRST : 512] = ra_ref[0:cut].astype(jnp.float32).reshape(8 * cut, 128)
    me = lax.axis_index("tp")
    wide[...] = jnp.zeros((12, 256, 128), jnp.float32)
    for i in range(4):
        peer = lax.bitwise_xor(me, i)
        for l in range(2):
            for j in range(3):
                for k in range(2):
                    rows = asc[pl.ds(128 * peer + 8 * k + 3 * l + j, 8, stride=16), :]
                    rows = adapter_scale * jnp.concatenate([rows[4:8], rows[0:4]], axis=0)
                    for h in range(2):
                        wide[6 * l + 3 * h + j, pl.ds(64 * i + 4 * l + 2 * h + k, 8, stride=8), :] = rows
    for n in range(12):
        left_ref[n] = wide[n].T.astype(jnp.bfloat16)
    for l in range(2):
        for j in range(3):
            rows = slice(QBLK * j, QBLK * j + QBLK)
            for block in range(7):
                cols = slice(QBLK * block, QBLK * block + QBLK)
                scale = scale_ref[j, l : l + 1, block : block + 1]
                frozen_ref[l, rows, cols] = codes_ref[l, rows, cols].astype(jnp.float32) * scale


def merge_kernel(left_ref, b0, b1, b2, b3, frozen_ref, *refs):
    state_in, out_hbm, peak_hbm, state_out = refs[:6], refs[6], refs[7], refs[8:14]
    out_ref, peak_ref, sems = refs[14:]
    states = [
        pltpu.make_async_copy(a, b, sems.at[6 + i])
        for i, (a, b) in enumerate(zip(state_in, state_out))
    ]
    for copy in states:
        copy.start()
    lane = lax.broadcasted_iota(jnp.int32, (1, 7), 1)
    right = jnp.concatenate([b_ref[...].reshape(64, 512) for b_ref in (b0, b1, b2, b3)], axis=0)
    copies = []
    for l in range(2):
        for j in range(3):
            row = 3 * l + j
            peaks = jnp.zeros((1, 7), jnp.float32)
            rows = slice(QBLK * j, QBLK * j + QBLK)
            for h, width in enumerate((512, 384)):
                product = jnp.dot(
                    left_ref[6 * l + 3 * h + j],
                    right[:, 0:width],
                    preferred_element_type=jnp.float32,
                )
                for c in range(width // QBLK):
                    block = 4 * h + c
                    cols = slice(QBLK * block, QBLK * block + QBLK)
                    merged = frozen_ref[l, rows, cols] + product[:, QBLK * c : QBLK * c + QBLK]
                    peak = (
                        jnp.max(
                            jnp.max(jnp.abs(merged), axis=0, keepdims=True), axis=1, keepdims=True
                        )
                        + 1e-06
                    )
                    out_ref[l, rows, cols] = (merged * (1.0 / peak)).astype(jnp.bfloat16)
                    peaks = jnp.where(lane == block, peak, peaks)
            peak_ref[j, l : l + 1, :] = peaks
            copies.append(
                pltpu.make_async_copy(
                    out_ref.at[l, rows, :], out_hbm.at[l, rows, :], sems.at[row]
                )
            )
            copies[-1].start()
    copies.append(pltpu.make_async_copy(peak_ref, peak_hbm, sems.at[12]))
    copies[-1].start()
    for copy in states + copies:
        copy.wait()


def shards(ga, gb, pa, ma, va, pb, mb, vb, codes, scales):
    f32, bf16 = jnp.float32, jnp.bfloat16
    sds = jax.ShapeDtypeStruct
    a_state = [sds((24, 128), f32)] * 3
    b_state = [sds((2, 2, 896), f32)] * 3
    pa, ma, va = (a.reshape(24, 128) for a in (pa, ma, va))
    first = pl.pallas_call(
        first_kernel,
        out_shape=sds((8, 128), f32),
        out_specs=vmem(1)[0],
        compiler_params=SMALL,
        cost_estimate=pl.CostEstimate(flops=10**9, bytes_accessed=4096, transcendentals=0),
        name="first",
    )()
    messages = pl.pallas_call(
        pack_kernel,
        out_shape=sds((8, 8, 896), bf16),
        in_specs=vmem(3),
        out_specs=vmem(1)[0],
        scratch_shapes=[pltpu.VMEM((8, 8, 896), f32)],
        compiler_params=SMALL,
        cost_estimate=pl.CostEstimate(flops=10**9, bytes_accessed=400000, transcendentals=0),
        name="pack",
    )(ga.reshape(2, 96, 128), gb, first)
    received = lax.all_to_all(
        messages, "dp", 0, 0, tiled=True, axis_index_groups=[DP_ORDER]
    )
    pb, mb, vb, send_b = pl.pallas_call(
        adam_b_kernel,
        out_shape=b_state + [sds((8, 8, 512), bf16)],
        in_specs=vmem(4),
        out_specs=vmem(4),
        scratch_shapes=[pltpu.VMEM((8, 512), f32)],
        compiler_params=SMALL,
        cost_estimate=pl.CostEstimate(flops=100000, bytes_accessed=400000, transcendentals=3584),
        name="adam_b",
    )(received, pb, mb, vb)
    all_b = [lax.all_to_all(send_b, "dp", 0, 0, tiled=True, axis_index_groups=[DP_ORDER])]
    pa, ma, va, send_a = pl.pallas_call(
        adam_a_kernel,
        out_shape=a_state + [sds((64, 8, 128), bf16)],
        in_specs=vmem(5),
        out_specs=vmem(4),
        scratch_shapes=[pltpu.VMEM((4, 8, 128), f32)],
        compiler_params=SMALL,
        cost_estimate=pl.CostEstimate(flops=100000, bytes_accessed=200000, transcendentals=3072),
        name="adam_a",
    )(received, pa, ma, va, send_b)
    all_b[0], send_a = lax.optimization_barrier((all_b[0], send_a))
    all_a = lax.all_to_all(
        send_a, ("roll", "tp"), 0, 0, tiled=True, axis_index_groups=[PLANE_ORDER]
    )
    for i in range(1, 4):
        all_b.append(lax.ppermute(all_b[0], "tp", [(t, t ^ i) for t in range(4)]))
    left, frozen = pl.pallas_call(
        prepare_kernel,
        out_shape=[sds((12, 128, 256), bf16), sds((2, 384, 896), f32)],
        in_specs=vmem(3),
        out_specs=vmem(2),
        scratch_shapes=[pltpu.VMEM((512, 128), f32), pltpu.VMEM((12, 256, 128), f32)],
        compiler_params=SMALL,
        cost_estimate=pl.CostEstimate(flops=10**6, bytes_accessed=4000000, transcendentals=0),
        name="prepare",
    )(all_a, codes, scales.transpose(1, 0, 2))
    out, peaks, pa, ma, va, pb, mb, vb = pl.pallas_call(
        merge_kernel,
        out_shape=[sds((2, 384, 896), bf16), sds((3, 2, 7), f32)] + a_state + b_state,
        in_specs=vmem(12),
        out_specs=hbm(8),
        scratch_shapes=[
            pltpu.VMEM((2, 384, 896), bf16),
            pltpu.VMEM((3, 2, 7), f32),
            pltpu.SemaphoreType.DMA((13,)),
        ],
        compiler_params=SMALL,
        name="merge",
    )(left, *all_b, frozen, pa, ma, va, pb, mb, vb)
    return (
        out,
        peaks.transpose(1, 0, 2),
        pa.reshape(2, 1, 1536),
        ma.reshape(2, 1, 1536),
        va.reshape(2, 1, 1536),
        pb,
        mb,
        vb,
    )


def solution(mesh):
    in_specs = (
        P("dp", None, ("roll", "tp"), None),
        P("dp", None, "tp", "roll"),
        P(None, ("roll", "tp"), "dp"),
        P(None, ("roll", "tp"), "dp"),
        P(None, ("roll", "tp"), "dp"),
        P(None, ("tp", "dp"), "roll"),
        P(None, ("tp", "dp"), "roll"),
        P(None, ("tp", "dp"), "roll"),
        P(None, ("dp", "tp"), "roll"),
        P(None, ("dp", "tp"), "roll"),
    )
    out_specs = (
        P(None, ("dp", "tp"), "roll"),
        P(None, ("dp", "tp"), "roll"),
        P(None, ("roll", "tp"), "dp"),
        P(None, ("roll", "tp"), "dp"),
        P(None, ("roll", "tp"), "dp"),
        P(None, ("tp", "dp"), "roll"),
        P(None, ("tp", "dp"), "roll"),
        P(None, ("tp", "dp"), "roll"),
    )
    return jax.shard_map(shards, mesh=mesh, in_specs=in_specs, out_specs=out_specs, check_vma=False)
```

```python
import jax
import jax.numpy as jnp
from jax import lax
from jax.experimental import pallas as pl
from jax.experimental.pallas import tpu as pltpu
from jax.sharding import PartitionSpec as P

QBLK = 128
STEP = 100
adapter_scale = 0.5
learn_rate = 0.05
DP_ORDER = [(4 + i) % 8 for i in range(8)]
PLANE_FIRST = 56
PLANE_ORDER = [(PLANE_FIRST + i) % 64 for i in range(64)]
SMALL = pltpu.CompilerParams(vmem_limit_bytes=16 * 1024 * 1024)


def adam(param, gradient, first, second):
    first_new = 0.9 * first + 0.1 * gradient
    second_new = 0.999 * second + 0.001 * gradient * gradient
    corr_one = 1.0 - 0.9**STEP
    corr_two = 1.0 - 0.999**STEP
    param_new = param - learn_rate * (first_new / corr_one) / (
        jnp.sqrt(second_new / corr_two) + 1e-08
    )
    return param_new, first_new, second_new


def vmem(n):
    return [pl.BlockSpec(memory_space=pltpu.VMEM)] * n


def hbm(n):
    return [pl.BlockSpec(memory_space=pltpu.HBM)] * n


def first_kernel(o_ref):
    o_ref[...] = jnp.zeros((8, 128), jnp.float32)


def pack_kernel(ga_ref, gb_ref, order_ref, m_ref, scr):
    del order_ref
    scr[:, :, 768:896] = jnp.zeros((8, 8, 128), jnp.float32)
    for l in range(2):
        for j in range(3):
            for d in range(8):
                scr[DP_ORDER.index(d), 4 * l : 4 * l + 4, 128 * j : 128 * j + 128] = ga_ref[
                    l, pl.ds(12 * d + j, 4, stride=3), :
                ]
        for d in range(8):
            scr[DP_ORDER.index(d), 4 * l : 4 * l + 2, 384:896] = gb_ref[0, l, 2 * d : 2 * d + 2, 0:512]
            scr[DP_ORDER.index(d), 4 * l + 2 : 4 * l + 4, 384:768] = gb_ref[0, l, 2 * d : 2 * d + 2, 512:896]
    m_ref[...] = scr[...].astype(jnp.bfloat16)


def adam_a_kernel(r_ref, pa, ma, va, order_ref, oa, oma, ova, sa_ref, asc):
    del order_ref
    total = r_ref[0, :, 0:384].astype(jnp.float32)
    for d in range(1, 8):
        total = total + r_ref[d, :, 0:384].astype(jnp.float32)
    asc[...] = jnp.zeros((4, 8, 128), jnp.float32)
    for j in range(3):
        rows = pl.ds(j, 8, stride=3)
        p, m, v = adam(pa[rows, :], total[:, 128 * j : 128 * j + 128], ma[rows, :], va[rows, :])
        oa[rows, :] = p
        oma[rows, :] = m
        ova[rows, :] = v
        for l in range(2):
            for t in range(4):
                asc[t, 3 * l + j : 3 * l + j + 1, :] = p[4 * l + t : 4 * l + t + 1, :]
    block = asc[...].astype(jnp.bfloat16)
    for r in range(16):
        sa_ref[4 * r : 4 * r + 4] = block


def adam_b_kernel(r_ref, pb, mb, vb, ob, omb, ovb, sb_ref, bsc):
    total = r_ref[0, :, 384:896].astype(jnp.float32)
    for d in range(1, 8):
        total = total + r_ref[d, :, 384:896].astype(jnp.float32)
    bsc[...] = jnp.zeros((8, 512), jnp.float32)
    for l in range(2):
        for h, (lo, hi) in enumerate(((0, 512), (512, 896))):
            rows = slice(4 * l + 2 * h, 4 * l + 2 * h + 2)
            p, m, v = adam(
                pb[l, :, lo:hi],
                total[rows, 0 : hi - lo],
                mb[l, :, lo:hi],
                vb[l, :, lo:hi],
            )
            ob[l, :, lo:hi] = p
            omb[l, :, lo:hi] = m
            ovb[l, :, lo:hi] = v
            bsc[rows, 0 : hi - lo] = p
    block = bsc[...].astype(jnp.bfloat16)
    for i in range(8):
        sb_ref[i] = block


def prepare_kernel(ra_ref, codes_ref, scale_ref, left_ref, frozen_ref, asc, wide):
    cut = 64 - PLANE_FIRST
    asc[0 : 8 * PLANE_FIRST] = ra_ref[cut:64].astype(jnp.float32).reshape(8 * PLANE_FIRST, 128)
    asc[8 * PLANE_FIRST : 512] = ra_ref[0:cut].astype(jnp.float32).reshape(8 * cut, 128)
    me = lax.axis_index("tp")
    core = lax.rem(lax.axis_index("dp"), 2)
    steps = (0, 3 - core, 1, 2 + core)
    wide[...] = jnp.zeros((12, 256, 128), jnp.float32)
    for i in range(4):
        peer = lax.bitwise_xor(me, steps[i])
        for l in range(2):
            for j in range(3):
                for k in range(2):
                    rows = asc[pl.ds(128 * peer + 8 * k + 3 * l + j, 8, stride=16), :]
                    rows = adapter_scale * jnp.concatenate([rows[4:8], rows[0:4]], axis=0)
                    for h in range(2):
                        wide[6 * l + 3 * h + j, pl.ds(64 * i + 4 * l + 2 * h + k, 8, stride=8), :] = rows
    for n in range(12):
        left_ref[n] = wide[n].T.astype(jnp.bfloat16)
    for l in range(2):
        for j in range(3):
            rows = slice(QBLK * j, QBLK * j + QBLK)
            for block in range(7):
                cols = slice(QBLK * block, QBLK * block + QBLK)
                scale = scale_ref[j, l : l + 1, block : block + 1]
                frozen_ref[l, rows, cols] = codes_ref[l, rows, cols].astype(jnp.float32) * scale


def merge_kernel(left_ref, b0, b1, b2, b3, frozen_ref, *refs):
    state_in, out_hbm, peak_hbm, state_out = refs[:6], refs[6], refs[7], refs[8:14]
    out_ref, peak_ref, sems = refs[14:]
    states = [
        pltpu.make_async_copy(a, b, sems.at[6 + i])
        for i, (a, b) in enumerate(zip(state_in, state_out))
    ]
    for copy in states:
        copy.start()
    lane = lax.broadcasted_iota(jnp.int32, (1, 7), 1)
    right = jnp.concatenate([b_ref[...].reshape(64, 512) for b_ref in (b0, b1, b2, b3)], axis=0)
    copies = []
    for l in range(2):
        for j in range(3):
            row = 3 * l + j
            peaks = jnp.zeros((1, 7), jnp.float32)
            rows = slice(QBLK * j, QBLK * j + QBLK)
            for h, width in enumerate((512, 384)):
                product = jnp.dot(
                    left_ref[6 * l + 3 * h + j],
                    right[:, 0:width],
                    preferred_element_type=jnp.float32,
                )
                for c in range(width // QBLK):
                    block = 4 * h + c
                    cols = slice(QBLK * block, QBLK * block + QBLK)
                    merged = frozen_ref[l, rows, cols] + product[:, QBLK * c : QBLK * c + QBLK]
                    peak = (
                        jnp.max(
                            jnp.max(jnp.abs(merged), axis=0, keepdims=True), axis=1, keepdims=True
                        )
                        + 1e-06
                    )
                    out_ref[l, rows, cols] = (merged * (1.0 / peak)).astype(jnp.bfloat16)
                    peaks = jnp.where(lane == block, peak, peaks)
            peak_ref[j, l : l + 1, :] = peaks
            copies.append(
                pltpu.make_async_copy(
                    out_ref.at[l, rows, :], out_hbm.at[l, rows, :], sems.at[row]
                )
            )
            copies[-1].start()
    copies.append(pltpu.make_async_copy(peak_ref, peak_hbm, sems.at[12]))
    copies[-1].start()
    for copy in states + copies:
        copy.wait()


def shards(ga, gb, pa, ma, va, pb, mb, vb, codes, scales):
    f32, bf16 = jnp.float32, jnp.bfloat16
    sds = jax.ShapeDtypeStruct
    a_state = [sds((24, 128), f32)] * 3
    b_state = [sds((2, 2, 896), f32)] * 3
    pa, ma, va = (a.reshape(24, 128) for a in (pa, ma, va))
    first = pl.pallas_call(
        first_kernel,
        out_shape=sds((8, 128), f32),
        out_specs=vmem(1)[0],
        compiler_params=SMALL,
        cost_estimate=pl.CostEstimate(flops=10**9, bytes_accessed=4096, transcendentals=0),
        name="first",
    )()
    messages = pl.pallas_call(
        pack_kernel,
        out_shape=sds((8, 8, 896), bf16),
        in_specs=vmem(3),
        out_specs=vmem(1)[0],
        scratch_shapes=[pltpu.VMEM((8, 8, 896), f32)],
        compiler_params=SMALL,
        cost_estimate=pl.CostEstimate(flops=10**9, bytes_accessed=400000, transcendentals=0),
        name="pack",
    )(ga.reshape(2, 96, 128), gb, first)
    received = lax.all_to_all(
        messages, "dp", 0, 0, tiled=True, axis_index_groups=[DP_ORDER]
    )
    pb, mb, vb, send_b = pl.pallas_call(
        adam_b_kernel,
        out_shape=b_state + [sds((8, 8, 512), bf16)],
        in_specs=vmem(4),
        out_specs=vmem(4),
        scratch_shapes=[pltpu.VMEM((8, 512), f32)],
        compiler_params=SMALL,
        cost_estimate=pl.CostEstimate(flops=100000, bytes_accessed=400000, transcendentals=3584),
        name="adam_b",
    )(received, pb, mb, vb)
    all_b = [lax.all_to_all(send_b, "dp", 0, 0, tiled=True, axis_index_groups=[DP_ORDER])]
    pa, ma, va, send_a = pl.pallas_call(
        adam_a_kernel,
        out_shape=a_state + [sds((64, 8, 128), bf16)],
        in_specs=vmem(5),
        out_specs=vmem(4),
        scratch_shapes=[pltpu.VMEM((4, 8, 128), f32)],
        compiler_params=SMALL,
        cost_estimate=pl.CostEstimate(flops=100000, bytes_accessed=200000, transcendentals=3072),
        name="adam_a",
    )(received, pa, ma, va, send_b)
    all_b[0], send_a = lax.optimization_barrier((all_b[0], send_a))
    all_a = lax.all_to_all(
        send_a, ("roll", "tp"), 0, 0, tiled=True, axis_index_groups=[PLANE_ORDER]
    )
    far = [(4 * d + t, 4 * d + (t ^ (3 - d % 2))) for d in range(8) for t in range(4)]
    all_b.append(lax.ppermute(all_b[0], ("dp", "tp"), far))
    all_b.append(lax.ppermute(all_b[0], "tp", [(t, t ^ 1) for t in range(4)]))
    all_b.append(lax.ppermute(all_b[1], "dp", [(d, d ^ 1) for d in range(8)]))
    left, frozen = pl.pallas_call(
        prepare_kernel,
        out_shape=[sds((12, 128, 256), bf16), sds((2, 384, 896), f32)],
        in_specs=vmem(3),
        out_specs=vmem(2),
        scratch_shapes=[pltpu.VMEM((512, 128), f32), pltpu.VMEM((12, 256, 128), f32)],
        compiler_params=SMALL,
        cost_estimate=pl.CostEstimate(flops=10**6, bytes_accessed=4000000, transcendentals=0),
        name="prepare",
    )(all_a, codes, scales.transpose(1, 0, 2))
    out, peaks, pa, ma, va, pb, mb, vb = pl.pallas_call(
        merge_kernel,
        out_shape=[sds((2, 384, 896), bf16), sds((3, 2, 7), f32)] + a_state + b_state,
        in_specs=vmem(12),
        out_specs=hbm(8),
        scratch_shapes=[
            pltpu.VMEM((2, 384, 896), bf16),
            pltpu.VMEM((3, 2, 7), f32),
            pltpu.SemaphoreType.DMA((13,)),
        ],
        compiler_params=SMALL,
        name="merge",
    )(left, *all_b, frozen, pa, ma, va, pb, mb, vb)
    return (
        out,
        peaks.transpose(1, 0, 2),
        pa.reshape(2, 1, 1536),
        ma.reshape(2, 1, 1536),
        va.reshape(2, 1, 1536),
        pb,
        mb,
        vb,
    )


def solution(mesh):
    in_specs = (
        P("dp", None, ("roll", "tp"), None),
        P("dp", None, "tp", "roll"),
        P(None, ("roll", "tp"), "dp"),
        P(None, ("roll", "tp"), "dp"),
        P(None, ("roll", "tp"), "dp"),
        P(None, ("tp", "dp"), "roll"),
        P(None, ("tp", "dp"), "roll"),
        P(None, ("tp", "dp"), "roll"),
        P(None, ("dp", "tp"), "roll"),
        P(None, ("dp", "tp"), "roll"),
    )
    out_specs = (
        P(None, ("dp", "tp"), "roll"),
        P(None, ("dp", "tp"), "roll"),
        P(None, ("roll", "tp"), "dp"),
        P(None, ("roll", "tp"), "dp"),
        P(None, ("roll", "tp"), "dp"),
        P(None, ("tp", "dp"), "roll"),
        P(None, ("tp", "dp"), "roll"),
        P(None, ("tp", "dp"), "roll"),
    )
    return jax.shard_map(shards, mesh=mesh, in_specs=in_specs, out_specs=out_specs, check_vma=False)
```

```python
import jax
import jax.numpy as jnp
from jax import lax
from jax.experimental import pallas as pl
from jax.experimental.pallas import tpu as pltpu
from jax.sharding import PartitionSpec as P

QBLK = 128
STEP = 100
adapter_scale = 0.5
learn_rate = 0.05
DP_ORDER = [(4 + i) % 8 for i in range(8)]
PLANE_FIRST = 56
PLANE_ORDER = [(PLANE_FIRST + i) % 64 for i in range(64)]
SMALL = pltpu.CompilerParams(vmem_limit_bytes=16 * 1024 * 1024)


def adam(param, gradient, first, second):
    first_new = 0.9 * first + 0.1 * gradient
    second_new = 0.999 * second + 0.001 * gradient * gradient
    corr_one = 1.0 - 0.9**STEP
    corr_two = 1.0 - 0.999**STEP
    param_new = param - learn_rate * (first_new / corr_one) / (
        jnp.sqrt(second_new / corr_two) + 1e-08
    )
    return param_new, first_new, second_new


def vmem(n):
    return [pl.BlockSpec(memory_space=pltpu.VMEM)] * n


def hbm(n):
    return [pl.BlockSpec(memory_space=pltpu.HBM)] * n


def first_kernel(o_ref):
    o_ref[...] = jnp.zeros((8, 128), jnp.float32)


def pack_kernel(ga_ref, gb_ref, order_ref, m_ref, scr):
    del order_ref
    scr[:, :, 768:896] = jnp.zeros((8, 8, 128), jnp.float32)
    for l in range(2):
        for j in range(3):
            for d in range(8):
                scr[DP_ORDER.index(d), 4 * l : 4 * l + 4, 128 * j : 128 * j + 128] = ga_ref[
                    l, pl.ds(12 * d + j, 4, stride=3), :
                ]
        for d in range(8):
            scr[DP_ORDER.index(d), 4 * l : 4 * l + 2, 384:896] = gb_ref[0, l, 2 * d : 2 * d + 2, 0:512]
            scr[DP_ORDER.index(d), 4 * l + 2 : 4 * l + 4, 384:768] = gb_ref[0, l, 2 * d : 2 * d + 2, 512:896]
    m_ref[...] = scr[...].astype(jnp.bfloat16)


def adam_a_kernel(r_ref, pa, ma, va, order_ref, oa, oma, ova, sa_ref, asc):
    del order_ref
    total = r_ref[0, :, 0:384].astype(jnp.float32)
    for d in range(1, 8):
        total = total + r_ref[d, :, 0:384].astype(jnp.float32)
    asc[...] = jnp.zeros((4, 8, 128), jnp.float32)
    for j in range(3):
        rows = pl.ds(j, 8, stride=3)
        p, m, v = adam(pa[rows, :], total[:, 128 * j : 128 * j + 128], ma[rows, :], va[rows, :])
        oa[rows, :] = p
        oma[rows, :] = m
        ova[rows, :] = v
        for l in range(2):
            for t in range(4):
                asc[t, 3 * l + j : 3 * l + j + 1, :] = p[4 * l + t : 4 * l + t + 1, :]
    block = asc[...].astype(jnp.bfloat16)
    for r in range(16):
        sa_ref[4 * r : 4 * r + 4] = block


def adam_b_kernel(r_ref, pb, mb, vb, ob, omb, ovb, sb_ref, bsc):
    total = r_ref[0, :, 384:896].astype(jnp.float32)
    for d in range(1, 8):
        total = total + r_ref[d, :, 384:896].astype(jnp.float32)
    bsc[...] = jnp.zeros((8, 512), jnp.float32)
    for l in range(2):
        for h, (lo, hi) in enumerate(((0, 512), (512, 896))):
            rows = slice(4 * l + 2 * h, 4 * l + 2 * h + 2)
            p, m, v = adam(
                pb[l, :, lo:hi],
                total[rows, 0 : hi - lo],
                mb[l, :, lo:hi],
                vb[l, :, lo:hi],
            )
            ob[l, :, lo:hi] = p
            omb[l, :, lo:hi] = m
            ovb[l, :, lo:hi] = v
            bsc[rows, 0 : hi - lo] = p
    block = bsc[...].astype(jnp.bfloat16)
    for i in range(8):
        sb_ref[i] = block


def prepare_kernel(ra_ref, codes_ref, scale_ref, left_ref, frozen_ref, asc, part, wide):
    cut = 64 - PLANE_FIRST
    asc[0 : 8 * PLANE_FIRST] = ra_ref[cut:64].astype(jnp.float32).reshape(8 * PLANE_FIRST, 128)
    asc[8 * PLANE_FIRST : 512] = ra_ref[0:cut].astype(jnp.float32).reshape(8 * cut, 128)
    me = lax.axis_index("tp")
    core = lax.rem(lax.axis_index("dp"), 2)
    steps = (0, 3 - core, 1, 2 + core)
    wide[...] = jnp.zeros((12, 256, 128), jnp.float32)
    for i in range(4):
        peer = lax.bitwise_xor(me, steps[i])
        part[...] = asc[pl.ds(pl.multiple_of(128 * peer, 128), 128), :]
        for l in range(2):
            for j in range(3):
                for k in range(2):
                    rows = part[pl.ds(8 * k + 3 * l + j, 8, stride=16), :]
                    rows = adapter_scale * jnp.concatenate([rows[4:8], rows[0:4]], axis=0)
                    for h in range(2):
                        wide[6 * l + 3 * h + j, pl.ds(64 * i + 4 * l + 2 * h + k, 8, stride=8), :] = rows
    for n in range(12):
        left_ref[n] = wide[n].T.astype(jnp.bfloat16)
    for l in range(2):
        for j in range(3):
            rows = slice(QBLK * j, QBLK * j + QBLK)
            for block in range(7):
                cols = slice(QBLK * block, QBLK * block + QBLK)
                scale = scale_ref[j, l : l + 1, block : block + 1]
                frozen_ref[l, rows, cols] = codes_ref[l, rows, cols].astype(jnp.float32) * scale


def merge_kernel(left_ref, b0, b1, b2, b3, frozen_ref, *refs):
    state_in, out_hbm, peak_hbm, state_out = refs[:6], refs[6], refs[7], refs[8:14]
    out_ref, peak_ref, sems = refs[14:]
    states = [
        pltpu.make_async_copy(a, b, sems.at[6 + i])
        for i, (a, b) in enumerate(zip(state_in, state_out))
    ]
    for copy in states:
        copy.start()
    lane = lax.broadcasted_iota(jnp.int32, (1, 7), 1)
    right = jnp.concatenate([b_ref[...].reshape(64, 512) for b_ref in (b0, b1, b2, b3)], axis=0)
    copies = []
    for l in range(2):
        for j in range(3):
            row = 3 * l + j
            peaks = jnp.zeros((1, 7), jnp.float32)
            rows = slice(QBLK * j, QBLK * j + QBLK)
            for h, width in enumerate((512, 384)):
                product = jnp.dot(
                    left_ref[6 * l + 3 * h + j],
                    right[:, 0:width],
                    preferred_element_type=jnp.float32,
                )
                for c in range(width // QBLK):
                    block = 4 * h + c
                    cols = slice(QBLK * block, QBLK * block + QBLK)
                    merged = frozen_ref[l, rows, cols] + product[:, QBLK * c : QBLK * c + QBLK]
                    peak = (
                        jnp.max(
                            jnp.max(jnp.abs(merged), axis=0, keepdims=True), axis=1, keepdims=True
                        )
                        + 1e-06
                    )
                    out_ref[l, rows, cols] = (merged * (1.0 / peak)).astype(jnp.bfloat16)
                    peaks = jnp.where(lane == block, peak, peaks)
            peak_ref[j, l : l + 1, :] = peaks
            copies.append(
                pltpu.make_async_copy(
                    out_ref.at[l, rows, :], out_hbm.at[l, rows, :], sems.at[row]
                )
            )
            copies[-1].start()
    copies.append(pltpu.make_async_copy(peak_ref, peak_hbm, sems.at[12]))
    copies[-1].start()
    for copy in states + copies:
        copy.wait()


def shards(ga, gb, pa, ma, va, pb, mb, vb, codes, scales):
    f32, bf16 = jnp.float32, jnp.bfloat16
    sds = jax.ShapeDtypeStruct
    a_state = [sds((24, 128), f32)] * 3
    b_state = [sds((2, 2, 896), f32)] * 3
    pa, ma, va = (a.reshape(24, 128) for a in (pa, ma, va))
    first = pl.pallas_call(
        first_kernel,
        out_shape=sds((8, 128), f32),
        out_specs=vmem(1)[0],
        compiler_params=SMALL,
        cost_estimate=pl.CostEstimate(flops=10**9, bytes_accessed=4096, transcendentals=0),
        name="first",
    )()
    messages = pl.pallas_call(
        pack_kernel,
        out_shape=sds((8, 8, 896), bf16),
        in_specs=vmem(3),
        out_specs=vmem(1)[0],
        scratch_shapes=[pltpu.VMEM((8, 8, 896), f32)],
        compiler_params=SMALL,
        cost_estimate=pl.CostEstimate(flops=10**9, bytes_accessed=400000, transcendentals=0),
        name="pack",
    )(ga.reshape(2, 96, 128), gb, first)
    received = lax.all_to_all(
        messages, "dp", 0, 0, tiled=True, axis_index_groups=[DP_ORDER]
    )
    pb, mb, vb, send_b = pl.pallas_call(
        adam_b_kernel,
        out_shape=b_state + [sds((8, 8, 512), bf16)],
        in_specs=vmem(4),
        out_specs=vmem(4),
        scratch_shapes=[pltpu.VMEM((8, 512), f32)],
        compiler_params=SMALL,
        cost_estimate=pl.CostEstimate(flops=100000, bytes_accessed=400000, transcendentals=3584),
        name="adam_b",
    )(received, pb, mb, vb)
    all_b = [lax.all_to_all(send_b, "dp", 0, 0, tiled=True, axis_index_groups=[DP_ORDER])]
    pa, ma, va, send_a = pl.pallas_call(
        adam_a_kernel,
        out_shape=a_state + [sds((64, 8, 128), bf16)],
        in_specs=vmem(5),
        out_specs=vmem(4),
        scratch_shapes=[pltpu.VMEM((4, 8, 128), f32)],
        compiler_params=SMALL,
        cost_estimate=pl.CostEstimate(flops=100000, bytes_accessed=200000, transcendentals=3072),
        name="adam_a",
    )(received, pa, ma, va, send_b)
    all_b[0], send_a = lax.optimization_barrier((all_b[0], send_a))
    all_a = lax.all_to_all(
        send_a, ("roll", "tp"), 0, 0, tiled=True, axis_index_groups=[PLANE_ORDER]
    )
    far = [(4 * d + t, 4 * d + (t ^ (3 - d % 2))) for d in range(8) for t in range(4)]
    all_b.append(lax.ppermute(all_b[0], ("dp", "tp"), far))
    all_b.append(lax.ppermute(all_b[0], "tp", [(t, t ^ 1) for t in range(4)]))
    all_b.append(lax.ppermute(all_b[1], "dp", [(d, d ^ 1) for d in range(8)]))
    left, frozen = pl.pallas_call(
        prepare_kernel,
        out_shape=[sds((12, 128, 256), bf16), sds((2, 384, 896), f32)],
        in_specs=vmem(3),
        out_specs=vmem(2),
        scratch_shapes=[
            pltpu.VMEM((512, 128), f32),
            pltpu.VMEM((128, 128), f32),
            pltpu.VMEM((12, 256, 128), f32),
        ],
        compiler_params=SMALL,
        cost_estimate=pl.CostEstimate(flops=10**6, bytes_accessed=4000000, transcendentals=0),
        name="prepare",
    )(all_a, codes, scales.transpose(1, 0, 2))
    out, peaks, pa, ma, va, pb, mb, vb = pl.pallas_call(
        merge_kernel,
        out_shape=[sds((2, 384, 896), bf16), sds((3, 2, 7), f32)] + a_state + b_state,
        in_specs=vmem(12),
        out_specs=hbm(8),
        scratch_shapes=[
            pltpu.VMEM((2, 384, 896), bf16),
            pltpu.VMEM((3, 2, 7), f32),
            pltpu.SemaphoreType.DMA((13,)),
        ],
        compiler_params=SMALL,
        name="merge",
    )(left, *all_b, frozen, pa, ma, va, pb, mb, vb)
    return (
        out,
        peaks.transpose(1, 0, 2),
        pa.reshape(2, 1, 1536),
        ma.reshape(2, 1, 1536),
        va.reshape(2, 1, 1536),
        pb,
        mb,
        vb,
    )


def solution(mesh):
    in_specs = (
        P("dp", None, ("roll", "tp"), None),
        P("dp", None, "tp", "roll"),
        P(None, ("roll", "tp"), "dp"),
        P(None, ("roll", "tp"), "dp"),
        P(None, ("roll", "tp"), "dp"),
        P(None, ("tp", "dp"), "roll"),
        P(None, ("tp", "dp"), "roll"),
        P(None, ("tp", "dp"), "roll"),
        P(None, ("dp", "tp"), "roll"),
        P(None, ("dp", "tp"), "roll"),
    )
    out_specs = (
        P(None, ("dp", "tp"), "roll"),
        P(None, ("dp", "tp"), "roll"),
        P(None, ("roll", "tp"), "dp"),
        P(None, ("roll", "tp"), "dp"),
        P(None, ("roll", "tp"), "dp"),
        P(None, ("tp", "dp"), "roll"),
        P(None, ("tp", "dp"), "roll"),
        P(None, ("tp", "dp"), "roll"),
    )
    return jax.shard_map(shards, mesh=mesh, in_specs=in_specs, out_specs=out_specs, check_vma=False)
```

```python
import jax
import jax.numpy as jnp
from jax import lax
from jax.experimental import pallas as pl
from jax.experimental.pallas import tpu as pltpu
from jax.sharding import PartitionSpec as P

QBLK = 128
STEP = 100
adapter_scale = 0.5
learn_rate = 0.05
DP_ORDER = [(4 + i) % 8 for i in range(8)]
PLANE_FIRST = 56
PLANE_ORDER = [(PLANE_FIRST + i) % 64 for i in range(64)]
SMALL = pltpu.CompilerParams(vmem_limit_bytes=16 * 1024 * 1024)


def adam(param, gradient, first, second):
    first_new = 0.9 * first + 0.1 * gradient
    second_new = 0.999 * second + 0.001 * gradient * gradient
    corr_one = 1.0 - 0.9**STEP
    corr_two = 1.0 - 0.999**STEP
    param_new = param - learn_rate * (first_new / corr_one) / (
        jnp.sqrt(second_new / corr_two) + 1e-08
    )
    return param_new, first_new, second_new


def vmem(n):
    return [pl.BlockSpec(memory_space=pltpu.VMEM)] * n


def hbm(n):
    return [pl.BlockSpec(memory_space=pltpu.HBM)] * n


def first_kernel(o_ref):
    o_ref[...] = jnp.zeros((8, 128), jnp.float32)


def pack_kernel(ga_ref, gb_ref, order_ref, m_ref, scr):
    del order_ref
    scr[:, :, 768:896] = jnp.zeros((8, 8, 128), jnp.float32)
    for l in range(2):
        for j in range(3):
            for d in range(8):
                scr[DP_ORDER.index(d), 4 * l : 4 * l + 4, 128 * j : 128 * j + 128] = ga_ref[
                    l, pl.ds(12 * d + j, 4, stride=3), :
                ]
        for d in range(8):
            scr[DP_ORDER.index(d), 4 * l : 4 * l + 2, 384:896] = gb_ref[0, l, 2 * d : 2 * d + 2, 0:512]
            scr[DP_ORDER.index(d), 4 * l + 2 : 4 * l + 4, 384:768] = gb_ref[0, l, 2 * d : 2 * d + 2, 512:896]
    m_ref[...] = scr[...].astype(jnp.bfloat16)


def adam_a_kernel(r_ref, pa, ma, va, order_ref, oa, oma, ova, sa_ref, asc):
    del order_ref
    total = r_ref[0, :, 0:384].astype(jnp.float32)
    for d in range(1, 8):
        total = total + r_ref[d, :, 0:384].astype(jnp.float32)
    asc[...] = jnp.zeros((4, 8, 128), jnp.float32)
    for j in range(3):
        rows = pl.ds(j, 8, stride=3)
        p, m, v = adam(pa[rows, :], total[:, 128 * j : 128 * j + 128], ma[rows, :], va[rows, :])
        oa[rows, :] = p
        oma[rows, :] = m
        ova[rows, :] = v
        for l in range(2):
            for t in range(4):
                asc[t, 3 * l + j : 3 * l + j + 1, :] = p[4 * l + t : 4 * l + t + 1, :]
    block = asc[...].astype(jnp.bfloat16)
    for r in range(16):
        sa_ref[4 * r : 4 * r + 4] = block


def adam_b_kernel(r_ref, pb, mb, vb, ob, omb, ovb, sb_ref, bsc):
    total = r_ref[0, :, 384:896].astype(jnp.float32)
    for d in range(1, 8):
        total = total + r_ref[d, :, 384:896].astype(jnp.float32)
    bsc[...] = jnp.zeros((8, 512), jnp.float32)
    for l in range(2):
        for h, (lo, hi) in enumerate(((0, 512), (512, 896))):
            rows = slice(4 * l + 2 * h, 4 * l + 2 * h + 2)
            p, m, v = adam(
                pb[l, :, lo:hi],
                total[rows, 0 : hi - lo],
                mb[l, :, lo:hi],
                vb[l, :, lo:hi],
            )
            ob[l, :, lo:hi] = p
            omb[l, :, lo:hi] = m
            ovb[l, :, lo:hi] = v
            bsc[rows, 0 : hi - lo] = p
    block = bsc[...].astype(jnp.bfloat16)
    for i in range(8):
        sb_ref[i] = block


def prepare_kernel(ra_ref, codes_ref, scale_ref, left_ref, frozen_ref, asc, part, wide):
    cut = 64 - PLANE_FIRST
    asc[0 : 8 * PLANE_FIRST] = ra_ref[cut:64].astype(jnp.float32).reshape(8 * PLANE_FIRST, 128)
    asc[8 * PLANE_FIRST : 512] = ra_ref[0:cut].astype(jnp.float32).reshape(8 * cut, 128)
    me = lax.axis_index("tp")
    core = lax.rem(lax.axis_index("dp"), 2)
    steps = (0, 2 + core, 1, 3 - core)
    wide[...] = jnp.zeros((12, 256, 128), jnp.float32)
    for i in range(4):
        peer = lax.bitwise_xor(me, steps[i])
        part[...] = asc[pl.ds(pl.multiple_of(128 * peer, 128), 128), :]
        for l in range(2):
            for j in range(3):
                for k in range(2):
                    rows = part[pl.ds(8 * k + 3 * l + j, 8, stride=16), :]
                    rows = adapter_scale * jnp.concatenate([rows[4:8], rows[0:4]], axis=0)
                    for h in range(2):
                        wide[6 * l + 3 * h + j, pl.ds(64 * i + 4 * l + 2 * h + k, 8, stride=8), :] = rows
    for n in range(12):
        left_ref[n] = wide[n].T.astype(jnp.bfloat16)
    for l in range(2):
        for j in range(3):
            rows = slice(QBLK * j, QBLK * j + QBLK)
            for block in range(7):
                cols = slice(QBLK * block, QBLK * block + QBLK)
                scale = scale_ref[j, l : l + 1, block : block + 1]
                frozen_ref[l, rows, cols] = codes_ref[l, rows, cols].astype(jnp.float32) * scale


def merge_kernel(left_ref, b0, b1, b2, b3, frozen_ref, *refs):
    state_in, out_hbm, peak_hbm, state_out = refs[:6], refs[6], refs[7], refs[8:14]
    out_ref, peak_ref, sems = refs[14:]
    states = [
        pltpu.make_async_copy(a, b, sems.at[6 + i])
        for i, (a, b) in enumerate(zip(state_in, state_out))
    ]
    for copy in states:
        copy.start()
    lane = lax.broadcasted_iota(jnp.int32, (1, 7), 1)
    right = jnp.concatenate([b_ref[...].reshape(64, 512) for b_ref in (b0, b1, b2, b3)], axis=0)
    copies = []
    for l in range(2):
        for j in range(3):
            row = 3 * l + j
            peaks = jnp.zeros((1, 7), jnp.float32)
            rows = slice(QBLK * j, QBLK * j + QBLK)
            for h, width in enumerate((512, 384)):
                product = jnp.dot(
                    left_ref[6 * l + 3 * h + j],
                    right[:, 0:width],
                    preferred_element_type=jnp.float32,
                )
                for c in range(width // QBLK):
                    block = 4 * h + c
                    cols = slice(QBLK * block, QBLK * block + QBLK)
                    merged = frozen_ref[l, rows, cols] + product[:, QBLK * c : QBLK * c + QBLK]
                    peak = (
                        jnp.max(
                            jnp.max(jnp.abs(merged), axis=0, keepdims=True), axis=1, keepdims=True
                        )
                        + 1e-06
                    )
                    out_ref[l, rows, cols] = (merged * (1.0 / peak)).astype(jnp.bfloat16)
                    peaks = jnp.where(lane == block, peak, peaks)
            peak_ref[j, l : l + 1, :] = peaks
            copies.append(
                pltpu.make_async_copy(
                    out_ref.at[l, rows, :], out_hbm.at[l, rows, :], sems.at[row]
                )
            )
            copies[-1].start()
    copies.append(pltpu.make_async_copy(peak_ref, peak_hbm, sems.at[12]))
    copies[-1].start()
    for copy in states + copies:
        copy.wait()


def shards(ga, gb, pa, ma, va, pb, mb, vb, codes, scales):
    f32, bf16 = jnp.float32, jnp.bfloat16
    sds = jax.ShapeDtypeStruct
    a_state = [sds((24, 128), f32)] * 3
    b_state = [sds((2, 2, 896), f32)] * 3
    pa, ma, va = (a.reshape(24, 128) for a in (pa, ma, va))
    first = pl.pallas_call(
        first_kernel,
        out_shape=sds((8, 128), f32),
        out_specs=vmem(1)[0],
        compiler_params=SMALL,
        cost_estimate=pl.CostEstimate(flops=10**9, bytes_accessed=4096, transcendentals=0),
        name="first",
    )()
    messages = pl.pallas_call(
        pack_kernel,
        out_shape=sds((8, 8, 896), bf16),
        in_specs=vmem(3),
        out_specs=vmem(1)[0],
        scratch_shapes=[pltpu.VMEM((8, 8, 896), f32)],
        compiler_params=SMALL,
        cost_estimate=pl.CostEstimate(flops=10**9, bytes_accessed=400000, transcendentals=0),
        name="pack",
    )(ga.reshape(2, 96, 128), gb, first)
    received = lax.all_to_all(
        messages, "dp", 0, 0, tiled=True, axis_index_groups=[DP_ORDER]
    )
    pb, mb, vb, send_b = pl.pallas_call(
        adam_b_kernel,
        out_shape=b_state + [sds((8, 8, 512), bf16)],
        in_specs=vmem(4),
        out_specs=vmem(4),
        scratch_shapes=[pltpu.VMEM((8, 512), f32)],
        compiler_params=SMALL,
        cost_estimate=pl.CostEstimate(flops=100000, bytes_accessed=400000, transcendentals=3584),
        name="adam_b",
    )(received, pb, mb, vb)
    all_b = [lax.all_to_all(send_b, "dp", 0, 0, tiled=True, axis_index_groups=[DP_ORDER])]
    pa, ma, va, send_a = pl.pallas_call(
        adam_a_kernel,
        out_shape=a_state + [sds((64, 8, 128), bf16)],
        in_specs=vmem(5),
        out_specs=vmem(4),
        scratch_shapes=[pltpu.VMEM((4, 8, 128), f32)],
        compiler_params=SMALL,
        cost_estimate=pl.CostEstimate(flops=100000, bytes_accessed=200000, transcendentals=3072),
        name="adam_a",
    )(received, pa, ma, va, send_b)
    all_b[0], send_a = lax.optimization_barrier((all_b[0], send_a))
    all_a = lax.all_to_all(
        send_a, ("roll", "tp"), 0, 0, tiled=True, axis_index_groups=[PLANE_ORDER]
    )
    far = [(4 * d + t, 4 * d + (t ^ (2 + d % 2))) for d in range(8) for t in range(4)]
    all_b.append(lax.ppermute(all_b[0], ("dp", "tp"), far))
    all_b.append(lax.ppermute(all_b[0], "tp", [(t, t ^ 1) for t in range(4)]))
    all_b.append(lax.ppermute(all_b[1], "dp", [(d, d ^ 1) for d in range(8)]))
    left, frozen = pl.pallas_call(
        prepare_kernel,
        out_shape=[sds((12, 128, 256), bf16), sds((2, 384, 896), f32)],
        in_specs=vmem(3),
        out_specs=vmem(2),
        scratch_shapes=[
            pltpu.VMEM((512, 128), f32),
            pltpu.VMEM((128, 128), f32),
            pltpu.VMEM((12, 256, 128), f32),
        ],
        compiler_params=SMALL,
        cost_estimate=pl.CostEstimate(flops=10**6, bytes_accessed=4000000, transcendentals=0),
        name="prepare",
    )(all_a, codes, scales.transpose(1, 0, 2))
    out, peaks, pa, ma, va, pb, mb, vb = pl.pallas_call(
        merge_kernel,
        out_shape=[sds((2, 384, 896), bf16), sds((3, 2, 7), f32)] + a_state + b_state,
        in_specs=vmem(12),
        out_specs=hbm(8),
        scratch_shapes=[
            pltpu.VMEM((2, 384, 896), bf16),
            pltpu.VMEM((3, 2, 7), f32),
            pltpu.SemaphoreType.DMA((13,)),
        ],
        compiler_params=SMALL,
        name="merge",
    )(left, *all_b, frozen, pa, ma, va, pb, mb, vb)
    return (
        out,
        peaks.transpose(1, 0, 2),
        pa.reshape(2, 1, 1536),
        ma.reshape(2, 1, 1536),
        va.reshape(2, 1, 1536),
        pb,
        mb,
        vb,
    )


def solution(mesh):
    in_specs = (
        P("dp", None, ("roll", "tp"), None),
        P("dp", None, "tp", "roll"),
        P(None, ("roll", "tp"), "dp"),
        P(None, ("roll", "tp"), "dp"),
        P(None, ("roll", "tp"), "dp"),
        P(None, ("tp", "dp"), "roll"),
        P(None, ("tp", "dp"), "roll"),
        P(None, ("tp", "dp"), "roll"),
        P(None, ("dp", "tp"), "roll"),
        P(None, ("dp", "tp"), "roll"),
    )
    out_specs = (
        P(None, ("dp", "tp"), "roll"),
        P(None, ("dp", "tp"), "roll"),
        P(None, ("roll", "tp"), "dp"),
        P(None, ("roll", "tp"), "dp"),
        P(None, ("roll", "tp"), "dp"),
        P(None, ("tp", "dp"), "roll"),
        P(None, ("tp", "dp"), "roll"),
        P(None, ("tp", "dp"), "roll"),
    )
    return jax.shard_map(shards, mesh=mesh, in_specs=in_specs, out_specs=out_specs, check_vma=False)
```
